256 devices in a mesh: ma: 64 (over z, x, core), row: 4 (over y).
Axes of the slice: x: 4, y: 4, z: 8, core: 2. Of those that a mesh axis runs over, the one named last changes fastest.
Arguments:
- nonlinear: bfloat16 [128, 1536, 4, 512], P('ma', None, None, 'row'), may hold values from -6 to 6
- legendre: bfloat16 [128, 768, 2, 512], P('ma'), may hold values from -0.15625 to 0.15625
- inverse: bfloat16 [2, 512, 2, 512, 512], P(None, 'ma', None, 'row'), may hold values from -0.25 to 0.25
- orders: int32 [128], P('ma'), may hold values from 0 to 1023, as said below
Outputs:
- solved: bfloat16 [128, 2, 512, 4, 512], P('ma', None, None, None, 'row')
The draws below stay inside these ranges and needn't reach their ends.
Inputs may be any that keep to these rules, and one draw needn't show every extreme that they name: The orders are distinct; slots 2 i and 2 i + 1 hold m and 1023 - m with m < 512, so every index of ma holds whole pairs.
All inputs are finite; a program needn't handle non-finite values.
Results may differ from the reference program's by a relative error of at most 0.0059.
Values may be sent and summed in bfloat16 or wider, within the bound.
A program may use at most 128 MiB of HBM per device.

```python
import jax
import jax.numpy as jnp
from jax import lax

L = 1024
NTH = 1536
NR = 512
F = 2
FC = 4
M_TOT = 128


def draw_orders(key, part):
    key = jax.random.fold_in(key, 11)
    first_key, second_key = jax.random.split(key)
    pair_count = M_TOT // 2
    remaining = jax.random.permutation(first_key, L // 2 - 1)[:pair_count - 1].astype(jnp.int32) + 1
    lower = jnp.concatenate([jnp.zeros((1,), jnp.int32), remaining])
    lower = jax.random.permutation(second_key, lower).astype(jnp.int32)
    paired = jnp.stack([lower, L - 1 - lower], axis=1)
    return paired.reshape(M_TOT).astype(jnp.int32)


def shard_levels(rng, extent, cuts, least, high):
    loudness, own = 1.0, jax.random.fold_in(rng, 6)
    for dim, parts in cuts:
        draws = jnp.exp(jax.random.uniform(jax.random.fold_in(own, dim), (parts,), jnp.float32, least / len(cuts), high / len(cuts)))
        loudness = loudness * jnp.repeat(draws, extent[dim] // parts).reshape([-1 if axis == dim else 1 for axis in range(len(extent))])
    return loudness


def normal_values(stream_key, shape, spread, limit, cuts=(), held_as=jnp.bfloat16):
    entries = spread * jax.random.normal(stream_key, shape, jnp.float32)
    if cuts:
        entries = entries * shard_levels(stream_key, shape, cuts, -0.22, 0.18)
    return jnp.clip(entries, -limit, limit).astype(held_as)


def setup_inputs(seed: int = 0) -> dict:
    arg_keys = jax.random.split(jax.random.key(seed), 5)
    nonlinear = normal_values(arg_keys[0], (M_TOT, NTH, FC, NR), 1.0, 6.0, ((0, 64), (3, 4)))
    legendre = normal_values(arg_keys[1], (M_TOT, NTH // 2, 2, L // 2), NTH ** -0.5, 0.15625, ((0, 64),))
    inverse = normal_values(arg_keys[2], (2, L // 2, F, NR, NR), NR ** -0.5, 0.25, ((1, 64), (3, 4)))
    orders = draw_orders(jax.random.fold_in(arg_keys[4], 71), 0)
    return {"nonlinear": nonlinear, "legendre": legendre, "inverse": inverse, "orders": orders}


def analyse_order(operands):
    field_values, table_part, order_value = operands
    half_theta = field_values.shape[0] // 2
    part_count = field_values.shape[1]
    radial_count = field_values.shape[2]
    northern = field_values[:half_theta].astype(jnp.float32)
    southern = field_values[half_theta:][::-1].astype(jnp.float32)
    even_part = (northern + southern).astype(jnp.bfloat16).reshape(half_theta, part_count * radial_count)
    odd_part = (northern - southern).astype(jnp.bfloat16).reshape(half_theta, part_count * radial_count)
    half_degree = table_part.shape[2]
    degree_half = lax.iota(jnp.int32, half_degree)
    results = []
    for parity in range(2):
        chosen = jnp.where((order_value + parity) % 2 == 0, even_part, odd_part)
        product = jnp.dot(table_part[:, parity, :].T, chosen, preferred_element_type=jnp.float32)
        live_mask = (2 * degree_half + parity) >= order_value
        product = jnp.where(live_mask[:, None], product, 0.0)
        results.append(product.astype(jnp.bfloat16).reshape(half_degree, part_count, radial_count))
    return jnp.stack(results, axis=0)


def solve_degree(operands):
    coeff_slab, inverse_slab = operands
    order_total = coeff_slab.shape[0]
    field_count = inverse_slab.shape[1]
    radial_count = coeff_slab.shape[3]
    separated = coeff_slab.reshape(order_total, 2, field_count, 2, radial_count).astype(jnp.float32)
    result = jnp.einsum('pfrs,mpfks->mpfkr', inverse_slab.astype(jnp.float32), separated)
    return result.astype(jnp.bfloat16).reshape(order_total, 2, 2 * field_count, radial_count)


def reference(nonlinear, legendre, inverse, orders):
    coefficients = lax.map(analyse_order, (nonlinear, legendre, orders))
    by_degree = jnp.transpose(coefficients, (2, 0, 1, 3, 4))
    inverse_by_degree = jnp.transpose(inverse, (1, 0, 2, 3, 4))
    solved = lax.map(solve_degree, (by_degree, inverse_by_degree))
    return jnp.transpose(solved, (1, 2, 0, 3, 4))
```

```python
import jax
import jax.numpy as jnp
from jax import lax
from jax.experimental import pallas as pl
from jax.experimental.pallas import tpu as pltpu
from jax.sharding import PartitionSpec as P

MESH = pl.DeviceIdType.MESH
RING = (4, 3, 5, 2, 6, 1, 7)
ZN, ON, YN = 8, 8, 4
SLOTS, PARITIES, HALVES = 2, 2, 2
CHUNKS = PARITIES * HALVES
ROWS, LANES = 16, 128


def exchange_kernel(coef, inverse, out, held, gathered, solved, back, weights, zs, zr, ks, kr, ys, yr, ls, lr, ms, mr, own, load):
    me = lax.axis_index("ma")
    y = lax.axis_index("row")
    z, o = me // ON, lax.rem(me, ON)

    def z_peer(i):
        return {"ma": lax.rem(z + i, ZN) * ON + o}

    def o_peer(i):
        return {"ma": z * ON + lax.rem(o + i, ON)}

    def y_peer(i):
        return {"row": lax.rem(y + i, YN)}

    fetch = pltpu.make_async_copy(inverse, weights, load)
    fetch.start()

    barrier = pltpu.get_barrier_semaphore()
    for i in range(1, ZN):
        pl.semaphore_signal(barrier, inc=1, device_id=z_peer(i), device_id_type=MESH)
        pl.semaphore_signal(barrier, inc=1, device_id=o_peer(i), device_id_type=MESH)
    for i in (1, YN - 1):
        pl.semaphore_signal(barrier, inc=1, device_id=y_peer(i), device_id_type=MESH)
    pl.semaphore_wait(barrier, 2 * (ZN - 1) + 2)

    def remote(src, dst, s, r, device):
        return pltpu.make_async_remote_copy(src_ref=src, dst_ref=dst, send_sem=s, recv_sem=r, device_id=device, device_id_type=MESH)

    def z_out(k, i):
        p, h = k // HALVES, k % HALVES
        there = lax.rem(z + i, ZN)
        return remote(coef.at[:, p, pl.ds(there * ON, ON), h], held.at[k, z], zs.at[k, i], zr.at[k, i], z_peer(i))

    def z_own(k):
        p, h = k // HALVES, k % HALVES
        return pltpu.make_async_copy(coef.at[:, p, pl.ds(z * ON, ON), h], held.at[k, z], own.at[0, k])

    def o_out(k, i):
        there = lax.rem(o + i, ON)
        return remote(held.at[k, :, :, there], gathered.at[k, y, o], ks.at[k, i], kr.at[k, i], o_peer(i))

    def o_own(k):
        return pltpu.make_async_copy(held.at[k, :, :, o], gathered.at[k, y, o], own.at[1, k])

    def y_first(k, i):
        return remote(gathered.at[k, y], gathered.at[k, y], ys.at[k, i], yr.at[k, i], y_peer((1, YN - 1)[i]))

    def y_second(k, i):
        origin = lax.rem(y + (YN - 1, 1)[i], YN)
        part = gathered.at[k, origin, pl.ds((0, ON // 2)[i], ON // 2)]
        return remote(part, part, ys.at[k, 2 + i], yr.at[k, 2 + i], y_peer((1, YN - 1)[i]))

    def l_out(k, i):
        there = lax.rem(o + i, ON)
        return remote(solved.at[k, there], back.at[k, :, :, o], ls.at[k, i], lr.at[k, i], o_peer(i))

    def l_own(k):
        return pltpu.make_async_copy(solved.at[k, o], back.at[k, :, :, o], own.at[2, k])

    def m_out(k, i):
        p, h = k // HALVES, k % HALVES
        there = lax.rem(z + i, ZN)
        return remote(back.at[k, there], out.at[:, p, pl.ds(z * ON, ON), h], ms.at[k, i], mr.at[k, i], z_peer(i))

    def m_own(k):
        p, h = k // HALVES, k % HALVES
        return pltpu.make_async_copy(back.at[k, z], out.at[:, p, pl.ds(z * ON, ON), h], own.at[3, k])

    def solve(k):
        p, h = k // HALVES, k % HALVES
        row = lax.broadcasted_iota(jnp.int32, (1, ROWS, LANES), 1)

        @pl.loop(0, 2)
        def _(half):
            part = gathered[k, :, pl.ds(half * 4, 4)]
            flat = part.reshape(YN, 4 * ZN * SLOTS * ROWS, LANES)
            left = jnp.concatenate([flat[0], flat[1], flat[2], flat[3]], axis=1)
            total = None
            for jl in range(4):
                right = weights[p, h * 4 + jl].reshape(2 * LANES, YN * LANES)
                product = lax.dot_general(left, right, (((1,), (1,)), ((), ())), preferred_element_type=jnp.float32)
                product = product.reshape(4 * ZN * SLOTS, ROWS, 2 * LANES)
                for f in range(2):
                    piece = product[:, :, f * LANES:(f + 1) * LANES]
                    piece = jnp.where(row // 2 == jl * 2 + f, piece, 0.0)
                    total = piece if total is None else total + piece
            solved[k, pl.ds(half * 4, 4)] = total.astype(jnp.bfloat16).reshape(4, ZN, SLOTS, ROWS, LANES)

    for k in range(CHUNKS):
        for i in RING:
            z_out(k, i).start()
        z_own(k).start()

    def stage_o(k):
        z_own(k).wait()
        for i in range(1, ZN):
            z_out(k, i).wait_recv()
        for i in range(1, ON):
            o_out(k, i).start()
        o_own(k).start()

    def stage_y(k):
        o_own(k).wait()
        for i in range(1, ON):
            o_out(k, i).wait_recv()
        for i in range(2):
            y_first(k, i).start()

    def stage_f(k):
        for i in range(2):
            y_first(k, i).wait_recv()
            y_second(k, i).start()

    def stage_s(k):
        if k == 0:
            fetch.wait()
        for i in range(2):
            y_second(k, i).wait_recv()
        solve(k)
        for i in range(1, ON):
            l_out(k, i).start()
        l_own(k).start()

    def stage_m(k):
        l_own(k).wait()
        for i in range(1, ON):
            l_out(k, i).wait_recv()
        for i in RING:
            m_out(k, i).start()
        m_own(k).start()

    stages = (stage_o, stage_y, stage_f, stage_s, stage_m)
    for step in range(CHUNKS + len(stages) - 1):
        for n, stage in enumerate(stages):
            if 0 <= step - n < CHUNKS:
                stage(step - n)

    for k in range(CHUNKS):
        m_own(k).wait()
        for i in range(1, ZN):
            m_out(k, i).wait_recv()
    for k in range(CHUNKS):
        for i in range(1, ZN):
            z_out(k, i).wait_send()
            o_out(k, i).wait_send()
            l_out(k, i).wait_send()
            m_out(k, i).wait_send()
        for i in range(2):
            y_first(k, i).wait_send()
            y_second(k, i).wait_send()


def exchange(coef, inverse):
    tile = (ROWS, LANES)
    dma = pltpu.SemaphoreType.DMA
    return pl.pallas_call(
        exchange_kernel,
        out_shape=jax.ShapeDtypeStruct(coef.shape, coef.dtype),
        in_specs=[pl.BlockSpec(memory_space=pl.ANY)] * 2,
        out_specs=pl.BlockSpec(memory_space=pl.ANY),
        scratch_shapes=[
            pltpu.VMEM((CHUNKS, ZN, SLOTS, ON) + tile, jnp.bfloat16),
            pltpu.VMEM((CHUNKS, YN, ON, ZN, SLOTS) + tile, jnp.bfloat16),
            pltpu.VMEM((CHUNKS, ON, ZN, SLOTS) + tile, jnp.bfloat16),
            pltpu.VMEM((CHUNKS, ZN, SLOTS, ON) + tile, jnp.bfloat16),
            pltpu.VMEM(inverse.shape, jnp.bfloat16),
            dma((CHUNKS, ZN)), dma((CHUNKS, ZN)),
            dma((CHUNKS, ON)), dma((CHUNKS, ON)),
            dma((CHUNKS, 4)), dma((CHUNKS, 4)),
            dma((CHUNKS, ON)), dma((CHUNKS, ON)),
            dma((CHUNKS, ZN)), dma((CHUNKS, ZN)),
            dma((4, CHUNKS)),
            dma,
        ],
        compiler_params=pltpu.CompilerParams(collective_id=0, has_side_effects=True, vmem_limit_bytes=48 * 1024 * 1024),
    )(coef, inverse)


def per_device(nonlinear, legendre, inverse, orders):
    order_count, theta_count, part_count, radial_rows = nonlinear.shape
    half_theta = theta_count // 2
    half_degree = legendre.shape[3]
    flattened = nonlinear.reshape(order_count, theta_count, part_count * radial_rows)
    northern = flattened[:, :half_theta].astype(jnp.float32)
    southern = flattened[:, half_theta:][:, ::-1].astype(jnp.float32)
    even_part = (northern + southern).astype(jnp.bfloat16)
    odd_part = (northern - southern).astype(jnp.bfloat16)
    degree_half = lax.iota(jnp.int32, half_degree)

    def analyse(parity):
        chosen = jnp.where(((orders + parity) % 2 == 0)[:, None, None], even_part, odd_part)
        table_part = legendre[:, :, parity, :]
        product = jnp.einsum("mhj,mhx->mjx", table_part, chosen, preferred_element_type=jnp.float32)
        live_mask = 2 * degree_half[None, :] + parity >= orders[:, None]
        product = jnp.where(live_mask[:, :, None], product, 0.0)
        return product.astype(jnp.bfloat16).reshape(
            order_count, 1, half_degree, part_count, radial_rows
        )

    coefficients = jnp.concatenate([analyse(0), analyse(1)], axis=1)
    coef = coefficients.reshape(SLOTS, PARITIES, ZN * ON, HALVES, ROWS, LANES)
    return exchange(coef, inverse).reshape(coefficients.shape)


def solution(mesh):
    in_specs = (
        P("ma", None, None, "row"),
        P("ma", None, None, None),
        P(None, "ma", None, "row", None),
        P("ma"),
    )
    out_specs = P("ma", None, None, None, "row")
    return jax.shard_map(
        per_device, mesh=mesh, in_specs=in_specs, out_specs=out_specs, check_vma=False
    )
```

```python
import jax
import jax.numpy as jnp
from jax import lax
from jax.experimental import pallas as pl
from jax.experimental.pallas import tpu as pltpu
from jax.sharding import PartitionSpec as P

MESH = pl.DeviceIdType.MESH
RING = (4, 3, 5, 2, 6, 1, 7)
ZN, ON, YN = 8, 8, 4
SLOTS, PARITIES, HALVES, QUAD = 2, 2, 2, 4
PER_SLOT = PARITIES * HALVES
CHUNKS = SLOTS * PER_SLOT
ROWS, LANES = 16, 128
PARTS = 4
THETA, FOLD = 768, 256
DEGREES = 512
BLOCKS = DEGREES // LANES


def kernel(orders, nonlinear, legendre, inverse, out,
           raw, wide, folded, table, stage, coef, held, gathered, solved, back, weights, zeros,
           zs, zr, ks, kr, ys, yr, ls, lr, ms, mr, own, load, fill):
    me = lax.axis_index("ma")
    y = lax.axis_index("row")
    z, o = me // ON, lax.rem(me, ON)
    upper = z >= ZN // 2

    def z_peer(i):
        return {"ma": lax.rem(z + i, ZN) * ON + o}

    def o_peer(i):
        return {"ma": z * ON + lax.rem(o + i, ON)}

    def y_peer(i):
        return {"row": lax.rem(y + i, YN)}

    fetches = []
    for slot in range(SLOTS):
        fetches.append(pltpu.make_async_copy(nonlinear.at[slot], raw.at[slot, 0], load.at[2 * slot]))
        fetches.append(pltpu.make_async_copy(legendre.at[slot], raw.at[slot, 1], load.at[2 * slot + 1]))
    fetches.append(pltpu.make_async_copy(inverse, weights, load.at[2 * SLOTS]))
    for fetch in fetches:
        fetch.start()

    barrier = pltpu.get_barrier_semaphore()
    for i in range(1, ZN):
        pl.semaphore_signal(barrier, inc=1, device_id=z_peer(i), device_id_type=MESH)
        pl.semaphore_signal(barrier, inc=1, device_id=o_peer(i), device_id_type=MESH)
    for i in (1, YN - 1):
        pl.semaphore_signal(barrier, inc=1, device_id=y_peer(i), device_id_type=MESH)

    def remote(src, dst, s, r, device):
        return pltpu.make_async_remote_copy(src_ref=src, dst_ref=dst, send_sem=s, recv_sem=r, device_id=device, device_id_type=MESH)

    def where(k):
        inner = k % PER_SLOT
        return k // PER_SLOT, inner // HALVES, inner % HALVES

    def z_out(k, i):
        slot, p, h = where(k)
        there = lax.rem(z + i, ZN)
        return remote(coef.at[slot, p, pl.ds(there * ON, ON), h], held.at[k, z], zs.at[k, i], zr.at[k, i], z_peer(i))

    def z_own(k):
        slot, p, h = where(k)
        return pltpu.make_async_copy(coef.at[slot, p, pl.ds(z * ON, ON), h], held.at[k, z], own.at[0, k])

    def o_out(k, i):
        there = lax.rem(o + i, ON)
        return remote(held.at[k, :, there], gathered.at[k, y, o], ks.at[k, i], kr.at[k, i], o_peer(i))

    def o_own(k):
        return pltpu.make_async_copy(held.at[k, :, o], gathered.at[k, y, o], own.at[1, k])

    def y_first(k, i):
        return remote(gathered.at[k, y], gathered.at[k, y], ys.at[k, i], yr.at[k, i], y_peer((1, YN - 1)[i]))

    def y_second(k, i):
        origin = lax.rem(y + (YN - 1, 1)[i], YN)
        part = gathered.at[k, origin, pl.ds((0, ON // 2)[i], ON // 2)]
        return remote(part, part, ys.at[k, 2 + i], yr.at[k, 2 + i], y_peer((1, YN - 1)[i]))

    def l_out(k, i):
        there = lax.rem(o + i, ON)
        return remote(solved.at[k, there], back.at[k, :, o], ls.at[k, i], lr.at[k, i], o_peer(i))

    def l_own(k):
        return pltpu.make_async_copy(solved.at[k, o], back.at[k, :, o], own.at[2, k])

    def m_out(k, i):
        slot, p, h = where(k)
        there = lax.rem(z + i, ZN)
        return remote(back.at[k, there], out.at[slot, p, pl.ds(z * ON, ON), h], ms.at[k, i], mr.at[k, i], z_peer(i))

    def m_own(k):
        slot, p, h = where(k)
        return pltpu.make_async_copy(back.at[k, z], out.at[slot, p, pl.ds(z * ON, ON), h], own.at[3, k])

    def fold(slot):
        fetches[2 * slot].wait()
        wide[...] = raw[slot, 0].astype(jnp.float32)
        index = lax.broadcasted_iota(jnp.int32, (FOLD, FOLD), 0) + lax.broadcasted_iota(jnp.int32, (FOLD, FOLD), 1)
        flip = (index == FOLD - 1).astype(jnp.bfloat16)
        sign = jnp.where(orders[slot] % 2 == 0, 1.0, -1.0).astype(jnp.float32)

        def rows(block):
            return [wide[pl.ds(block * FOLD * PARTS + c, FOLD, stride=PARTS), :] for c in range(PARTS)]

        for b in range(THETA // FOLD):
            north = jnp.concatenate(rows(b), axis=1)
            south = jnp.concatenate([v.astype(jnp.bfloat16) for v in rows(2 * THETA // FOLD - 1 - b)], axis=1)
            south = jnp.dot(flip, south, preferred_element_type=jnp.float32) * sign
            folded[0, b * FOLD:(b + 1) * FOLD, :] = (north + south).astype(jnp.bfloat16)
            folded[1, b * FOLD:(b + 1) * FOLD, :] = (north - south).astype(jnp.bfloat16)

    def tabulate(slot):
        fetches[2 * slot + 1].wait()
        wide[...] = raw[slot, 1].astype(jnp.float32)
        for p in range(PARITIES):
            for b in range(BLOCKS):
                table[p, :, b * LANES:(b + 1) * LANES] = wide[pl.ds(b * PARITIES + p, THETA, stride=BLOCKS * PARITIES), :].astype(jnp.bfloat16)

    def analyse(slot, p):
        product = lax.dot_general(table[p], folded[p], (((0,), (0,)), ((), ())), preferred_element_type=jnp.float32)
        degree = 2 * lax.broadcasted_iota(jnp.int32, (DEGREES, 1), 0) + p
        product = jnp.where(degree >= orders[slot], product, 0.0)
        for c in range(PARTS):
            stage[pl.ds(c, DEGREES, stride=PARTS), :] = product[:, c * LANES:(c + 1) * LANES]
        coef[slot, p] = stage[...].astype(jnp.bfloat16).reshape(ZN * ON, HALVES, ROWS, LANES)

    def solve(k):
        slot, p, h = where(k)
        row = lax.broadcasted_iota(jnp.int32, (1, ROWS, LANES), 1)
        flat = gathered[k].reshape(YN, ON * ZN * ROWS, LANES)
        left = jnp.concatenate([flat[n] for n in range(YN)], axis=1)
        total = None
        for jl in range(QUAD):
            right = weights[p, h * QUAD + jl].reshape(2 * LANES, YN * LANES)
            product = lax.dot_general(left, right, (((1,), (1,)), ((), ())), preferred_element_type=jnp.float32)
            product = product.reshape(ON * ZN, ROWS, 2 * LANES)
            for f in range(2):
                piece = product[:, :, f * LANES:(f + 1) * LANES]
                total = piece if total is None else jnp.where(row // 2 == jl * 2 + f, piece, total)
        solved[k] = total.astype(jnp.bfloat16).reshape(ON, ZN, ROWS, LANES)

    def stage_z(k):
        slot = k // PER_SLOT
        for i in RING:
            if slot == 0:
                z_out(k, i).start()
            else:
                @pl.when(lax.rem(z + i, ZN) >= ZN // 2)
                def _():
                    z_out(k, i).start()
        if slot == 0:
            z_own(k).start()
        else:
            @pl.when(upper)
            def _():
                z_own(k).start()

    def stage_o(k):
        z_own(k).wait()
        for i in range(1, ZN):
            z_out(k, i).wait_recv()
        for i in range(1, ON):
            o_out(k, i).start()
        o_own(k).start()

    def stage_y(k):
        o_own(k).wait()
        for i in range(1, ON):
            o_out(k, i).wait_recv()
        for i in range(2):
            y_first(k, i).start()

    def stage_f(k):
        for i in range(2):
            y_first(k, i).wait_recv()
            y_second(k, i).start()

    def stage_s(k):
        for i in range(1, ON):
            o_out(k, i).wait_send()
        for i in range(2):
            y_second(k, i).wait_recv()
        solve(k)
        for i in range(1, ON):
            l_out(k, i).start()
        l_own(k).start()

    def stage_m(k):
        for i in range(2):
            y_first(k, i).wait_send()
            y_second(k, i).wait_send()
        l_own(k).wait()
        for i in range(1, ON):
            l_out(k, i).wait_recv()
        for i in RING:
            m_out(k, i).start()
        m_own(k).start()

    fold(0)
    tabulate(0)
    analyse(0, 0)
    pl.semaphore_wait(barrier, 2 * (ZN - 1) + 2)
    stage_z(0)
    stage_z(1)
    analyse(0, 1)
    stage_z(2)
    stage_z(3)
    zeros[...] = jnp.zeros_like(zeros)
    fills = [pltpu.make_async_copy(zeros, out.at[1, n // HALVES, pl.ds(0, ZN * ON // 2), n % HALVES], fill.at[n]) for n in range(PER_SLOT)]
    for copy in fills:
        copy.start()
    fold(1)
    tabulate(1)
    stage_o(0)
    analyse(1, 0)
    stage_z(4)
    stage_z(5)
    analyse(1, 1)
    stage_z(6)
    stage_z(7)
    fetches[2 * SLOTS].wait()

    @pl.loop(0, CHUNKS + 3)
    def _(step):
        for stage_of, lag in ((stage_y, 0), (stage_o, -1), (stage_f, 1), (stage_s, 2), (stage_m, 3)):
            k = step - lag
            valid = jnp.logical_and(k >= 0, k < CHUNKS)
            live = jnp.logical_or(k < PER_SLOT, upper)

            @pl.when(jnp.logical_and(valid, live))
            def _():
                stage_of(k)

    for copy in fills:
        copy.wait()
    for k in range(CHUNKS):
        slot = k // PER_SLOT

        def sent():
            for i in range(1, ON):
                l_out(k, i).wait_send()
                m_out(k, i).wait_send()

        if slot == 0:
            for i in range(1, ZN):
                z_out(k, i).wait_send()
            sent()
        else:
            for i in range(1, ZN):
                @pl.when(lax.rem(z + i, ZN) >= ZN // 2)
                def _():
                    z_out(k, i).wait_send()
            pl.when(upper)(sent)
    for k in range(CHUNKS):
        if k < PER_SLOT:
            m_own(k).wait()
            for i in range(1, ZN):
                m_out(k, i).wait_recv()
        else:
            @pl.when(upper)
            def _():
                m_own(k).wait()
            for i in range(1, ZN):
                @pl.when(lax.rem(z + ZN - i, ZN) >= ZN // 2)
                def _():
                    m_out(k, i).wait_recv()


def per_device(nonlinear, legendre, inverse, orders):
    tile = (ROWS, LANES)
    dma = pltpu.SemaphoreType.DMA
    field = nonlinear.reshape(SLOTS, 2 * THETA * PARTS, LANES)
    values = legendre.reshape(SLOTS, THETA, PARITIES, BLOCKS, LANES).transpose(0, 1, 3, 2, 4)
    values = values.reshape(SLOTS, THETA * BLOCKS * PARITIES, LANES)
    solved = pl.pallas_call(
        kernel,
        out_shape=jax.ShapeDtypeStruct((SLOTS, PARITIES, ZN * ON, HALVES) + tile, jnp.bfloat16),
        in_specs=[pl.BlockSpec(memory_space=pltpu.SMEM)] + [pl.BlockSpec(memory_space=pl.ANY)] * 3,
        out_specs=pl.BlockSpec(memory_space=pl.ANY),
        scratch_shapes=[
            pltpu.VMEM((SLOTS, 2) + field.shape[1:], jnp.bfloat16),
            pltpu.VMEM(field.shape[1:], jnp.float32),
            pltpu.VMEM((PARITIES, THETA, PARTS * LANES), jnp.bfloat16),
            pltpu.VMEM((PARITIES, THETA, DEGREES), jnp.bfloat16),
            pltpu.VMEM((DEGREES * PARTS, LANES), jnp.float32),
            pltpu.VMEM((SLOTS, PARITIES, ZN * ON, HALVES) + tile, jnp.bfloat16),
            pltpu.VMEM((CHUNKS, ZN, ON) + tile, jnp.bfloat16),
            pltpu.VMEM((CHUNKS, YN, ON, ZN) + tile, jnp.bfloat16),
            pltpu.VMEM((CHUNKS, ON, ZN) + tile, jnp.bfloat16),
            pltpu.VMEM((CHUNKS, ZN, ON) + tile, jnp.bfloat16),
            pltpu.VMEM(inverse.shape, jnp.bfloat16),
            pltpu.VMEM((ZN * ON // 2,) + tile, jnp.bfloat16),
            dma((CHUNKS, ZN)), dma((CHUNKS, ZN)),
            dma((CHUNKS, ON)), dma((CHUNKS, ON)),
            dma((CHUNKS, 4)), dma((CHUNKS, 4)),
            dma((CHUNKS, ON)), dma((CHUNKS, ON)),
            dma((CHUNKS, ZN)), dma((CHUNKS, ZN)),
            dma((4, CHUNKS)),
            dma((2 * SLOTS + 1,)),
            dma((PER_SLOT,)),
        ],
        compiler_params=pltpu.CompilerParams(collective_id=0, has_side_effects=True, vmem_limit_bytes=52 * 1024 * 1024),
    )(orders, field, values, inverse)
    return solved.reshape(SLOTS, PARITIES, DEGREES, PARTS, LANES)


def solution(mesh):
    in_specs = (
        P("ma", None, None, "row"),
        P("ma", None, None, None),
        P(None, "ma", None, "row", None),
        P("ma"),
    )
    out_specs = P("ma", None, None, None, "row")
    return jax.shard_map(
        per_device, mesh=mesh, in_specs=in_specs, out_specs=out_specs, check_vma=False
    )
```

```python
import jax
import jax.numpy as jnp
from jax import lax
from jax.experimental import pallas as pl
from jax.experimental.pallas import tpu as pltpu
from jax.sharding import PartitionSpec as P

MESH = pl.DeviceIdType.MESH
RING = (4, 3, 5, 2, 6, 1, 7)
ZN, ON, YN = 8, 8, 4
MA = ZN * ON
SLOTS, PARITIES, HALVES, QUAD = 2, 2, 2, 4
PER_SLOT = PARITIES * HALVES
CHUNKS = SLOTS * PER_SLOT
ROWS, LANES = 16, 128
Z_AHEAD, F_LAG, S_LAG = 4, 1, 2
PARTS = 4
THETA, FOLD = 768, 256
DEGREES = 512
BLOCKS = DEGREES // LANES


def kernel(orders, nonlinear, legendre, inverse, out,
           raw, wide, folded, table, stage, coef, gathered, solved, weights, zeros,
           zs, zr, ys, yr, ms, mr, own, load, fill):
    me = lax.axis_index("ma")
    y = lax.axis_index("row")
    z, o = me // ON, lax.rem(me, ON)
    upper = z >= ZN // 2

    def y_peer(i):
        return {"row": lax.rem(y + i, YN)}

    fetches = []
    for slot in range(SLOTS):
        fetches.append(pltpu.make_async_copy(nonlinear.at[slot], raw.at[slot, 0], load.at[2 * slot]))
        fetches.append(pltpu.make_async_copy(legendre.at[slot], raw.at[slot, 1], load.at[2 * slot + 1]))
    fetches.append(pltpu.make_async_copy(inverse, weights, load.at[2 * SLOTS]))
    for fetch in fetches:
        fetch.start()

    barrier = pltpu.get_barrier_semaphore()

    @pl.loop(1, MA)
    def _(i):
        pl.semaphore_signal(barrier, inc=1, device_id={"ma": lax.rem(me + i, MA)}, device_id_type=MESH)

    for i in (1, YN - 1):
        pl.semaphore_signal(barrier, inc=1, device_id=y_peer(i), device_id_type=MESH)

    def remote(src, dst, s, r, device):
        return pltpu.make_async_remote_copy(src_ref=src, dst_ref=dst, send_sem=s, recv_sem=r, device_id=device, device_id_type=MESH)

    def where(k):
        inner = k % PER_SLOT
        return k // PER_SLOT, inner // HALVES, inner % HALVES

    def z_out(k, there):
        slot, p, h = where(k)
        return remote(coef.at[slot, p, there, h], gathered.at[k, y, me], zs.at[k], zr.at[k], {"ma": there})

    def z_own(k):
        slot, p, h = where(k)
        return pltpu.make_async_copy(coef.at[slot, p, me, h], gathered.at[k, y, me], own.at[0, k])

    def y_first(k, i):
        return remote(gathered.at[k, y], gathered.at[k, y], ys.at[k, i], yr.at[k, i], y_peer((1, YN - 1)[i]))

    def y_second(k, i):
        origin = lax.rem(y + (YN - 1, 1)[i], YN)
        part = gathered.at[k, origin, pl.ds((0, MA // 2)[i], MA // 2)]
        return remote(part, part, ys.at[k, 2 + i], yr.at[k, 2 + i], y_peer((1, YN - 1)[i]))

    def m_out(k, there):
        slot, p, h = where(k)
        return remote(solved.at[k, there], out.at[slot, p, me, h], ms.at[k], mr.at[k], {"ma": there})

    def m_own(k):
        slot, p, h = where(k)
        return pltpu.make_async_copy(solved.at[k, me], out.at[slot, p, me, h], own.at[1, k])

    def drain(sem, count):
        part = solved.at[0, pl.ds(0, count)]
        pltpu.make_async_copy(part, part, sem).wait()

    def to_all(copy, k):
        @pl.loop(0, ON)
        def _(i):
            beside = lax.rem(o + i, ON)
            for n in RING:
                copy(k, lax.rem(z + n, ZN) * ON + beside).start()

            @pl.when(i > 0)
            def _():
                copy(k, z * ON + beside).start()

    def to_upper(copy, k):
        @pl.loop(0, ON)
        def _(i):
            beside = lax.rem(o + i, ON)
            for n in range(ZN // 2):
                there = (ZN // 2 + lax.rem(z + n, ZN // 2)) * ON + beside

                @pl.when(there != me)
                def _():
                    copy(k, there).start()

    def fold(slot):
        fetches[2 * slot].wait()
        wide[...] = raw[slot, 0].astype(jnp.float32)
        index = lax.broadcasted_iota(jnp.int32, (FOLD, FOLD), 0) + lax.broadcasted_iota(jnp.int32, (FOLD, FOLD), 1)
        flip = (index == FOLD - 1).astype(jnp.bfloat16)
        sign = jnp.where(orders[slot] % 2 == 0, 1.0, -1.0).astype(jnp.float32)

        def rows(block):
            return [wide[pl.ds(block * FOLD * PARTS + c, FOLD, stride=PARTS), :] for c in range(PARTS)]

        for b in range(THETA // FOLD):
            north = jnp.concatenate(rows(b), axis=1)
            south = jnp.concatenate([v.astype(jnp.bfloat16) for v in rows(2 * THETA // FOLD - 1 - b)], axis=1)
            south = jnp.dot(flip, south, preferred_element_type=jnp.float32) * sign
            folded[0, b * FOLD:(b + 1) * FOLD, :] = (north + south).astype(jnp.bfloat16)
            folded[1, b * FOLD:(b + 1) * FOLD, :] = (north - south).astype(jnp.bfloat16)

    def tabulate(slot):
        fetches[2 * slot + 1].wait()
        wide[...] = raw[slot, 1].astype(jnp.float32)
        for p in range(PARITIES):
            for b in range(BLOCKS):
                table[p, :, b * LANES:(b + 1) * LANES] = wide[pl.ds(b * PARITIES + p, THETA, stride=BLOCKS * PARITIES), :].astype(jnp.bfloat16)

    def analyse(slot, p):
        product = lax.dot_general(table[p], folded[p], (((0,), (0,)), ((), ())), preferred_element_type=jnp.float32)
        degree = 2 * lax.broadcasted_iota(jnp.int32, (DEGREES, 1), 0) + p
        product = jnp.where(degree >= orders[slot], product, 0.0)
        for c in range(PARTS):
            stage[pl.ds(c, DEGREES, stride=PARTS), :] = product[:, c * LANES:(c + 1) * LANES]
        coef[slot, p] = stage[...].astype(jnp.bfloat16).reshape(MA, HALVES, ROWS, LANES)

    def solve(k):
        slot, p, h = where(k)
        row = lax.broadcasted_iota(jnp.int32, (1, ROWS, LANES), 1)
        flat = gathered[k].reshape(YN, MA * ROWS, LANES)
        left = jnp.concatenate([flat[n] for n in range(YN)], axis=1)
        total = None
        for jl in range(QUAD):
            right = weights[p, h * QUAD + jl].reshape(2 * LANES, YN * LANES)
            product = lax.dot_general(left, right, (((1,), (1,)), ((), ())), preferred_element_type=jnp.float32)
            product = product.reshape(MA, ROWS, 2 * LANES)
            for f in range(2):
                piece = product[:, :, f * LANES:(f + 1) * LANES]
                total = piece if total is None else jnp.where(row // 2 == jl * 2 + f, piece, total)
        solved[k] = total.astype(jnp.bfloat16).reshape(MA, ROWS, LANES)

    def stage_z(k):
        @pl.when(k < PER_SLOT)
        def _():
            to_all(z_out, k)
            z_own(k).start()

        @pl.when(k >= PER_SLOT)
        def _():
            to_upper(z_out, k)

            @pl.when(upper)
            def _():
                z_own(k).start()

    def stage_y(k):
        z_own(k).wait()
        drain(zr.at[k], MA - 1)
        for i in range(2):
            y_first(k, i).start()

    def stage_f(k):
        for i in range(2):
            y_first(k, i).wait_recv()
            y_second(k, i).start()

    def stage_s(k):
        for i in range(2):
            y_second(k, i).wait_recv()
        solve(k)
        to_all(m_out, k)
        m_own(k).start()

    fold(0)
    tabulate(0)
    analyse(0, 0)
    pl.semaphore_wait(barrier, MA - 1 + 2)
    stage_z(0)
    stage_z(1)
    analyse(0, 1)
    for k in range(2, Z_AHEAD):
        stage_z(k)
    zeros[...] = jnp.zeros_like(zeros)
    fills = [pltpu.make_async_copy(zeros, out.at[1, n // HALVES, pl.ds(0, MA // 2), n % HALVES], fill.at[n]) for n in range(PER_SLOT)]
    for copy in fills:
        copy.start()
    fold(1)
    tabulate(1)
    analyse(1, 0)
    analyse(1, 1)
    fetches[2 * SLOTS].wait()

    @pl.loop(0, CHUNKS + S_LAG)
    def _(step):
        @pl.when(step + Z_AHEAD < CHUNKS)
        def _():
            stage_z(step + Z_AHEAD)

        for stage_of, lag in ((stage_y, 0), (stage_f, F_LAG), (stage_s, S_LAG)):
            k = step - lag
            valid = jnp.logical_and(k >= 0, k < CHUNKS)
            live = jnp.logical_or(k < PER_SLOT, upper)

            @pl.when(jnp.logical_and(valid, live))
            def _():
                stage_of(k)

    for copy in fills:
        copy.wait()

    @pl.loop(0, CHUNKS)
    def _(k):
        def returned():
            for i in range(2):
                y_first(k, i).wait_send()
                y_second(k, i).wait_send()
            drain(ms.at[k], MA - 1)
            m_own(k).wait()

        @pl.when(k < PER_SLOT)
        def _():
            drain(zs.at[k], MA - 1)
            returned()
            drain(mr.at[k], MA - 1)

        @pl.when(jnp.logical_and(k >= PER_SLOT, upper))
        def _():
            drain(zs.at[k], MA // 2 - 1)
            returned()
            drain(mr.at[k], MA // 2 - 1)

        @pl.when(jnp.logical_and(k >= PER_SLOT, jnp.logical_not(upper)))
        def _():
            drain(zs.at[k], MA // 2)
            drain(mr.at[k], MA // 2)


def per_device(nonlinear, legendre, inverse, orders):
    tile = (ROWS, LANES)
    dma = pltpu.SemaphoreType.DMA
    field = nonlinear.reshape(SLOTS, 2 * THETA * PARTS, LANES)
    values = legendre.reshape(SLOTS, THETA, PARITIES, BLOCKS, LANES).transpose(0, 1, 3, 2, 4)
    values = values.reshape(SLOTS, THETA * BLOCKS * PARITIES, LANES)
    solved = pl.pallas_call(
        kernel,
        out_shape=jax.ShapeDtypeStruct((SLOTS, PARITIES, MA, HALVES) + tile, jnp.bfloat16),
        in_specs=[pl.BlockSpec(memory_space=pltpu.SMEM)] + [pl.BlockSpec(memory_space=pl.ANY)] * 3,
        out_specs=pl.BlockSpec(memory_space=pl.ANY),
        scratch_shapes=[
            pltpu.VMEM((SLOTS, 2) + field.shape[1:], jnp.bfloat16),
            pltpu.VMEM(field.shape[1:], jnp.float32),
            pltpu.VMEM((PARITIES, THETA, PARTS * LANES), jnp.bfloat16),
            pltpu.VMEM((PARITIES, THETA, DEGREES), jnp.bfloat16),
            pltpu.VMEM((DEGREES * PARTS, LANES), jnp.float32),
            pltpu.VMEM((SLOTS, PARITIES, MA, HALVES) + tile, jnp.bfloat16),
            pltpu.VMEM((CHUNKS, YN, MA) + tile, jnp.bfloat16),
            pltpu.VMEM((CHUNKS, MA) + tile, jnp.bfloat16),
            pltpu.VMEM(inverse.shape, jnp.bfloat16),
            pltpu.VMEM((MA // 2,) + tile, jnp.bfloat16),
            dma((CHUNKS,)), dma((CHUNKS,)),
            dma((CHUNKS, 4)), dma((CHUNKS, 4)),
            dma((CHUNKS,)), dma((CHUNKS,)),
            dma((2, CHUNKS)),
            dma((2 * SLOTS + 1,)),
            dma((PER_SLOT,)),
        ],
        compiler_params=pltpu.CompilerParams(collective_id=0, has_side_effects=True, vmem_limit_bytes=52 * 1024 * 1024),
    )(orders, field, values, inverse)
    return solved.reshape(SLOTS, PARITIES, DEGREES, PARTS, LANES)


def solution(mesh):
    in_specs = (
        P("ma", None, None, "row"),
        P("ma", None, None, None),
        P(None, "ma", None, "row", None),
        P("ma"),
    )
    out_specs = P("ma", None, None, None, "row")
    return jax.shard_map(
        per_device, mesh=mesh, in_specs=in_specs, out_specs=out_specs, check_vma=False
    )
```

```python
import jax
import jax.numpy as jnp
from jax import lax
from jax.experimental import pallas as pl
from jax.experimental.pallas import tpu as pltpu
from jax.sharding import PartitionSpec as P

MESH = pl.DeviceIdType.MESH
NEAR, FAR = (0, 1, 7, 2), (6, 3, 5, 4)
OFFSETS = NEAR + FAR
GROUPS, SIDE = 2, 4
ZN, ON, YN = 8, 8, 4
MA = ZN * ON
SLOTS, PARITIES, HALVES, QUAD = 2, 2, 2, 4
PER_SLOT = PARITIES * HALVES
CHUNKS = SLOTS * PER_SLOT
ROWS, LANES = 16, 128
Z_AHEAD, F_LAG, S_LAG = 4, 1, 2
PIECES = CHUNKS * GROUPS
LAST = PIECES - GROUPS
PARTS = 4
THETA, FOLD = 768, 256
DEGREES = 512
BLOCKS = DEGREES // LANES


def kernel(orders, nonlinear, legendre, inverse, out,
           raw, wide, folded, table, stage, coef, gathered, solved, weights, zeros,
           zs, zr, ys, yr, ms, mr, own, load, fill):
    me = lax.axis_index("ma")
    y = lax.axis_index("row")
    z, o = me // ON, lax.rem(me, ON)
    upper = z >= ZN // 2

    def y_peer(i):
        return {"row": lax.rem(y + i, YN)}

    fetches = []
    for slot in range(SLOTS):
        fetches.append(pltpu.make_async_copy(nonlinear.at[slot], raw.at[slot, 0], load.at[2 * slot]))
        fetches.append(pltpu.make_async_copy(legendre.at[slot], raw.at[slot, 1], load.at[2 * slot + 1]))
    fetches.append(pltpu.make_async_copy(inverse, weights, load.at[2 * SLOTS]))
    for fetch in fetches[:2]:
        fetch.start()

    barrier = pltpu.get_barrier_semaphore()

    @pl.loop(1, MA)
    def _(i):
        pl.semaphore_signal(barrier, inc=1, device_id={"ma": lax.rem(me + i, MA)}, device_id_type=MESH)

    for i in (1, YN - 1):
        pl.semaphore_signal(barrier, inc=1, device_id=y_peer(i), device_id_type=MESH)

    def remote(src, dst, s, r, device):
        return pltpu.make_async_remote_copy(src_ref=src, dst_ref=dst, send_sem=s, recv_sem=r, device_id=device, device_id_type=MESH)

    def where(k):
        inner = k % PER_SLOT
        return k // PER_SLOT, inner // HALVES, inner % HALVES

    def z_out(k, q, beside):
        slot, p, h = where(k)
        away = (ZN - OFFSETS[q]) % ZN
        there = lax.rem(z + away, ZN) * ON + beside
        return remote(coef.at[slot, p, there, h], gathered.at[k, y, q // SIDE, q % SIDE, o], zs.at[k], zr.at[k, q // SIDE], {"ma": there})

    def z_own(k):
        slot, p, h = where(k)
        return pltpu.make_async_copy(coef.at[slot, p, me, h], gathered.at[k, y, 0, 0, o], own.at[0, k])

    def y_first(k, g, i):
        part = gathered.at[k, y, g]
        return remote(part, part, ys.at[k, g, i], yr.at[k, g, i], y_peer((1, YN - 1)[i]))

    def y_second(k, g, i):
        origin = lax.rem(y + (YN - 1, 1)[i], YN)
        part = gathered.at[k, origin, g, pl.ds((0, SIDE // 2)[i], SIDE // 2)]
        return remote(part, part, ys.at[k, g, 2 + i], yr.at[k, g, 2 + i], y_peer((1, YN - 1)[i]))

    def m_out(k, g, r, beside):
        slot, p, h = where(k)
        away = NEAR[r] + g * (FAR[r] - NEAR[r])
        there = lax.rem(z + away, ZN) * ON + beside
        return remote(solved.at[k, g, r, beside], out.at[slot, p, me, h], ms.at[k], mr.at[k], {"ma": there})

    def m_own(k):
        slot, p, h = where(k)
        return pltpu.make_async_copy(solved.at[k, 0, 0, o], out.at[slot, p, me, h], own.at[1, k])

    def drain(sem, count):
        part = coef.at[0, 0, pl.ds(0, count), 0]
        pltpu.make_async_copy(part, part, sem).wait()

    def fold(slot):
        fetches[2 * slot].wait()
        wide[...] = raw[slot, 0].astype(jnp.float32)
        index = lax.broadcasted_iota(jnp.int32, (FOLD, FOLD), 0) + lax.broadcasted_iota(jnp.int32, (FOLD, FOLD), 1)
        flip = (index == FOLD - 1).astype(jnp.bfloat16)
        sign = jnp.where(orders[slot] % 2 == 0, 1.0, -1.0).astype(jnp.float32)

        def rows(block):
            return [wide[pl.ds(block * FOLD * PARTS + c, FOLD, stride=PARTS), :] for c in range(PARTS)]

        for b in range(THETA // FOLD):
            north = jnp.concatenate(rows(b), axis=1)
            south = jnp.concatenate([v.astype(jnp.bfloat16) for v in rows(2 * THETA // FOLD - 1 - b)], axis=1)
            south = jnp.dot(flip, south, preferred_element_type=jnp.float32) * sign
            folded[0, b * FOLD:(b + 1) * FOLD, :] = (north + south).astype(jnp.bfloat16)
            folded[1, b * FOLD:(b + 1) * FOLD, :] = (north - south).astype(jnp.bfloat16)

    def widen(slot):
        fetches[2 * slot + 1].wait()
        wide[...] = raw[slot, 1].astype(jnp.float32)

    def tabulate(p):
        for b in range(BLOCKS):
            table[p, :, b * LANES:(b + 1) * LANES] = wide[pl.ds(b * PARITIES + p, THETA, stride=BLOCKS * PARITIES), :].astype(jnp.bfloat16)

    def analyse(slot, p):
        product = lax.dot_general(table[p], folded[p], (((0,), (0,)), ((), ())), preferred_element_type=jnp.float32)
        degree = 2 * lax.broadcasted_iota(jnp.int32, (DEGREES, 1), 0) + p
        product = jnp.where(degree >= orders[slot], product, 0.0)
        for c in range(PARTS):
            stage[pl.ds(c, DEGREES, stride=PARTS), :] = product[:, c * LANES:(c + 1) * LANES]
        coef[slot, p] = stage[...].astype(jnp.bfloat16).reshape(MA, HALVES, ROWS, LANES)

    def solve(k, g):
        slot, p, h = where(k)
        row = lax.broadcasted_iota(jnp.int32, (1, ROWS, LANES), 1)
        flat = gathered[k, :, g].reshape(YN, SIDE * ON * ROWS, LANES)
        left = jnp.concatenate([flat[n] for n in range(YN)], axis=1)
        total = None
        for jl in range(QUAD):
            right = weights[p, h * QUAD + jl].reshape(2 * LANES, YN * LANES)
            product = lax.dot_general(left, right, (((1,), (1,)), ((), ())), preferred_element_type=jnp.float32)
            product = product.reshape(SIDE * ON, ROWS, 2 * LANES)
            for f in range(2):
                piece = product[:, :, f * LANES:(f + 1) * LANES]
                total = piece if total is None else jnp.where(row // 2 == jl * 2 + f, piece, total)
        solved[k, g] = total.astype(jnp.bfloat16).reshape(SIDE, ON, ROWS, LANES)

    def stage_z(k):
        for g in range(GROUPS):
            @pl.loop(0, ON)
            def _(i):
                beside = lax.rem(o + i, ON)
                for r in range(SIDE):
                    q = g * SIDE + r
                    lands = lax.rem(z + (ZN - OFFSETS[q]) % ZN, ZN)
                    go = jnp.logical_or(k < PER_SLOT, lands >= ZN // 2)
                    if q == 0:
                        go = jnp.logical_and(go, i > 0)

                    @pl.when(go)
                    def _():
                        z_out(k, q, beside).start()

        @pl.when(jnp.logical_or(k < PER_SLOT, upper))
        def _():
            z_own(k).start()

    def stage_y(k, g):
        @pl.when(g == 0)
        def _():
            z_own(k).wait()
            drain(zr.at[k, 0], SIDE * ON - 1)

        @pl.when(g == 1)
        def _():
            drain(zr.at[k, 1], SIDE * ON)

        for i in range(2):
            y_first(k, g, i).start()

    def stage_f(k, g):
        for i in range(2):
            y_first(k, g, i).wait_recv()
            y_second(k, g, i).start()

    def stage_s(k, g):
        for i in range(2):
            y_second(k, g, i).wait_recv()
        solve(k, g)

        @pl.loop(0, ON)
        def _(i):
            beside = lax.rem(o + i, ON)
            for r in range(SIDE):
                if r == 0:
                    @pl.when(g + i > 0)
                    def _():
                        m_out(k, g, r, beside).start()
                else:
                    m_out(k, g, r, beside).start()

        @pl.when(g == 0)
        def _():
            m_own(k).start()

    fold(0)
    widen(0)
    for fetch in fetches[2:]:
        fetch.start()
    tabulate(0)
    analyse(0, 0)
    pl.semaphore_wait(barrier, MA - 1 + 2)
    stage_z(0)
    stage_z(1)
    tabulate(1)
    analyse(0, 1)
    for k in range(2, Z_AHEAD):
        stage_z(k)
    zeros[...] = jnp.zeros_like(zeros)
    fills = [pltpu.make_async_copy(zeros, out.at[1, n // HALVES, pl.ds(0, MA // 2), n % HALVES], fill.at[n]) for n in range(PER_SLOT)]
    for copy in fills:
        copy.start()
    stage_y(0, 0)
    fold(1)
    widen(1)
    tabulate(0)
    analyse(1, 0)
    tabulate(1)
    analyse(1, 1)
    fetches[2 * SLOTS].wait()

    @pl.loop(0, PIECES + S_LAG)
    def _(step):
        @pl.when(jnp.logical_and(lax.rem(step, GROUPS) == 0, step // GROUPS + Z_AHEAD < CHUNKS))
        def _():
            stage_z(step // GROUPS + Z_AHEAD)

        for stage_of, lag in ((stage_y, 0), (stage_f, F_LAG), (stage_s, S_LAG)):
            t = step - lag
            k = t // GROUPS
            g = lax.rem(t + t // LAST, GROUPS)
            valid = jnp.logical_and(t >= (1 if stage_of is stage_y else 0), t < PIECES)
            live = jnp.logical_or(k < PER_SLOT, upper)

            @pl.when(jnp.logical_and(valid, live))
            def _():
                stage_of(k, g)

    for copy in fills:
        copy.wait()

    @pl.loop(0, CHUNKS)
    def _(k):
        def returned():
            for g in range(GROUPS):
                for i in range(2):
                    y_first(k, g, i).wait_send()
                    y_second(k, g, i).wait_send()
            drain(ms.at[k], MA - 1)
            m_own(k).wait()

        @pl.when(k < PER_SLOT)
        def _():
            drain(zs.at[k], MA - 1)
            returned()
            drain(mr.at[k], MA - 1)

        @pl.when(jnp.logical_and(k >= PER_SLOT, upper))
        def _():
            drain(zs.at[k], MA // 2 - 1)
            returned()
            drain(mr.at[k], MA // 2 - 1)

        @pl.when(jnp.logical_and(k >= PER_SLOT, jnp.logical_not(upper)))
        def _():
            drain(zs.at[k], MA // 2)
            drain(mr.at[k], MA // 2)


def per_device(nonlinear, legendre, inverse, orders):
    tile = (ROWS, LANES)
    dma = pltpu.SemaphoreType.DMA
    field = nonlinear.reshape(SLOTS, 2 * THETA * PARTS, LANES)
    values = legendre.reshape(SLOTS, THETA, PARITIES, BLOCKS, LANES).transpose(0, 1, 3, 2, 4)
    values = values.reshape(SLOTS, THETA * BLOCKS * PARITIES, LANES)
    solved = pl.pallas_call(
        kernel,
        out_shape=jax.ShapeDtypeStruct((SLOTS, PARITIES, MA, HALVES) + tile, jnp.bfloat16),
        in_specs=[pl.BlockSpec(memory_space=pltpu.SMEM)] + [pl.BlockSpec(memory_space=pl.ANY)] * 3,
        out_specs=pl.BlockSpec(memory_space=pl.ANY),
        scratch_shapes=[
            pltpu.VMEM((SLOTS, 2) + field.shape[1:], jnp.bfloat16),
            pltpu.VMEM(field.shape[1:], jnp.float32),
            pltpu.VMEM((PARITIES, THETA, PARTS * LANES), jnp.bfloat16),
            pltpu.VMEM((PARITIES, THETA, DEGREES), jnp.bfloat16),
            pltpu.VMEM((DEGREES * PARTS, LANES), jnp.float32),
            pltpu.VMEM((SLOTS, PARITIES, MA, HALVES) + tile, jnp.bfloat16),
            pltpu.VMEM((CHUNKS, YN, GROUPS, SIDE, ON) + tile, jnp.bfloat16),
            pltpu.VMEM((CHUNKS, GROUPS, SIDE, ON) + tile, jnp.bfloat16),
            pltpu.VMEM(inverse.shape, jnp.bfloat16),
            pltpu.VMEM((MA // 2,) + tile, jnp.bfloat16),
            dma((CHUNKS,)), dma((CHUNKS, GROUPS)),
            dma((CHUNKS, GROUPS, 4)), dma((CHUNKS, GROUPS, 4)),
            dma((CHUNKS,)), dma((CHUNKS,)),
            dma((2, CHUNKS)),
            dma((2 * SLOTS + 1,)),
            dma((PER_SLOT,)),
        ],
        compiler_params=pltpu.CompilerParams(collective_id=0, has_side_effects=True, vmem_limit_bytes=52 * 1024 * 1024),
    )(orders, field, values, inverse)
    return solved.reshape(SLOTS, PARITIES, DEGREES, PARTS, LANES)


def solution(mesh):
    in_specs = (
        P("ma", None, None, "row"),
        P("ma", None, None, None),
        P(None, "ma", None, "row", None),
        P("ma"),
    )
    out_specs = P("ma", None, None, None, "row")
    return jax.shard_map(
        per_device, mesh=mesh, in_specs=in_specs, out_specs=out_specs, check_vma=False
    )
```

```python
import jax
import jax.numpy as jnp
from jax import lax
from jax.experimental import pallas as pl
from jax.experimental.pallas import tpu as pltpu
from jax.sharding import PartitionSpec as P

MESH = pl.DeviceIdType.MESH
NEAR, FAR = (0, 1, 7, 2), (6, 3, 5, 4)
OFFSETS = NEAR + FAR
GROUPS, SIDE = 2, 4
ZN, ON, YN = 8, 8, 4
MA = ZN * ON
SLOTS, PARITIES, HALVES, QUAD = 2, 2, 2, 4
PER_SLOT = PARITIES * HALVES
CHUNKS = SLOTS * PER_SLOT
ROWS, LANES = 16, 128
F_LAG, S_LAG = 1, 2
PIECES = CHUNKS * GROUPS
LAST = PIECES - GROUPS
PARTS = 4
THETA, FOLD = 768, 256
DEGREES = 512
BLOCKS = DEGREES // LANES


def kernel(orders, nonlinear, legendre, inverse, out,
           raw, wide, folded, table, stage, coef, gathered, solved, weights, zeros,
           zs, zr, ys, yr, ms, mr, own, load, fill):
    me = lax.axis_index("ma")
    y = lax.axis_index("row")
    z, o = me // ON, lax.rem(me, ON)
    upper = z >= ZN // 2

    def y_peer(i):
        return {"row": lax.rem(y + i, YN)}

    fetches = []
    for slot in range(SLOTS):
        fetches.append(pltpu.make_async_copy(nonlinear.at[slot], raw.at[slot, 0], load.at[2 * slot]))
        fetches.append(pltpu.make_async_copy(legendre.at[slot], raw.at[slot, 1], load.at[2 * slot + 1]))
    fetches.append(pltpu.make_async_copy(inverse, weights, load.at[2 * SLOTS]))
    for fetch in fetches[:2]:
        fetch.start()

    barrier = pltpu.get_barrier_semaphore()

    @pl.loop(1, MA)
    def _(i):
        pl.semaphore_signal(barrier, inc=1, device_id={"ma": lax.rem(me + i, MA)}, device_id_type=MESH)

    for i in (1, YN - 1):
        pl.semaphore_signal(barrier, inc=1, device_id=y_peer(i), device_id_type=MESH)

    def remote(src, dst, s, r, device):
        return pltpu.make_async_remote_copy(src_ref=src, dst_ref=dst, send_sem=s, recv_sem=r, device_id=device, device_id_type=MESH)

    def where(k):
        inner = k % PER_SLOT
        return k // PER_SLOT, inner // HALVES, inner % HALVES

    def z_out(k, q, beside):
        slot, p, h = where(k)
        away = (ZN - OFFSETS[q]) % ZN
        there = lax.rem(z + away, ZN) * ON + beside
        return remote(coef.at[slot, p, there, h], gathered.at[k, y, q // SIDE, q % SIDE, o], zs.at[k], zr.at[k, q // SIDE], {"ma": there})

    def z_own(k):
        slot, p, h = where(k)
        return pltpu.make_async_copy(coef.at[slot, p, me, h], gathered.at[k, y, 0, 0, o], own.at[0, k])

    def y_first(k, g, i):
        part = gathered.at[k, y, g]
        return remote(part, part, ys.at[k, g, i], yr.at[k, g, i], y_peer((1, YN - 1)[i]))

    def y_second(k, g, i):
        origin = lax.rem(y + (YN - 1, 1)[i], YN)
        part = gathered.at[k, origin, g, pl.ds((0, SIDE // 2)[i], SIDE // 2)]
        return remote(part, part, ys.at[k, g, 2 + i], yr.at[k, g, 2 + i], y_peer((1, YN - 1)[i]))

    def m_out(k, g, r, beside):
        slot, p, h = where(k)
        away = NEAR[r] + g * (FAR[r] - NEAR[r])
        there = lax.rem(z + away, ZN) * ON + beside
        return remote(solved.at[k, g, r, beside], out.at[slot, p, me, h], ms.at[k], mr.at[k], {"ma": there})

    def m_own(k):
        slot, p, h = where(k)
        return pltpu.make_async_copy(solved.at[k, 0, 0, o], out.at[slot, p, me, h], own.at[1, k])

    def drain(sem, count):
        part = coef.at[0, 0, pl.ds(0, count), 0]
        pltpu.make_async_copy(part, part, sem).wait()

    def fold(slot):
        fetches[2 * slot].wait()
        wide[...] = raw[slot, 0].astype(jnp.float32)
        index = lax.broadcasted_iota(jnp.int32, (FOLD, FOLD), 0) + lax.broadcasted_iota(jnp.int32, (FOLD, FOLD), 1)
        flip = (index == FOLD - 1).astype(jnp.bfloat16)
        sign = jnp.where(orders[slot] % 2 == 0, 1.0, -1.0).astype(jnp.float32)

        def rows(block):
            return [wide[pl.ds(block * FOLD * PARTS + c, FOLD, stride=PARTS), :] for c in range(PARTS)]

        for b in range(THETA // FOLD):
            north = jnp.concatenate(rows(b), axis=1)
            south = jnp.concatenate([v.astype(jnp.bfloat16) for v in rows(2 * THETA // FOLD - 1 - b)], axis=1)
            south = jnp.dot(flip, south, preferred_element_type=jnp.float32) * sign
            folded[0, b * FOLD:(b + 1) * FOLD, :] = (north + south).astype(jnp.bfloat16)
            folded[1, b * FOLD:(b + 1) * FOLD, :] = (north - south).astype(jnp.bfloat16)

    def widen(slot):
        fetches[2 * slot + 1].wait()
        wide[...] = raw[slot, 1].astype(jnp.float32)

    def tabulate(p):
        for b in range(BLOCKS):
            table[p, :, b * LANES:(b + 1) * LANES] = wide[pl.ds(b * PARITIES + p, THETA, stride=BLOCKS * PARITIES), :].astype(jnp.bfloat16)

    def analyse(slot, p):
        product = lax.dot_general(table[p], folded[p], (((0,), (0,)), ((), ())), preferred_element_type=jnp.float32)
        degree = 2 * lax.broadcasted_iota(jnp.int32, (DEGREES, 1), 0) + p
        product = jnp.where(degree >= orders[slot], product, 0.0)
        for c in range(PARTS):
            stage[pl.ds(c, DEGREES, stride=PARTS), :] = product[:, c * LANES:(c + 1) * LANES]
        coef[slot, p] = stage[...].astype(jnp.bfloat16).reshape(MA, HALVES, ROWS, LANES)

    def solve(k, g):
        slot, p, h = where(k)
        row = lax.broadcasted_iota(jnp.int32, (1, ROWS, LANES), 1)
        flat = gathered[k, :, g].reshape(YN, SIDE * ON * ROWS, LANES)
        left = jnp.concatenate([flat[n] for n in range(YN)], axis=1)
        total = None
        for jl in range(QUAD):
            right = weights[p, h * QUAD + jl].reshape(2 * LANES, YN * LANES)
            product = lax.dot_general(left, right, (((1,), (1,)), ((), ())), preferred_element_type=jnp.float32)
            product = product.reshape(SIDE * ON, ROWS, 2 * LANES)
            for f in range(2):
                piece = product[:, :, f * LANES:(f + 1) * LANES]
                total = piece if total is None else jnp.where(row // 2 == jl * 2 + f, piece, total)
        solved[k, g] = total.astype(jnp.bfloat16).reshape(SIDE, ON, ROWS, LANES)

    def stage_z(k):
        for g in range(GROUPS):
            @pl.loop(0, ON)
            def _(i):
                beside = lax.rem(o + i, ON)
                for r in range(SIDE):
                    q = g * SIDE + r
                    lands = lax.rem(z + (ZN - OFFSETS[q]) % ZN, ZN)
                    go = jnp.logical_or(k < PER_SLOT, lands >= ZN // 2)
                    if q == 0:
                        go = jnp.logical_and(go, i > 0)

                    @pl.when(go)
                    def _():
                        z_out(k, q, beside).start()

        @pl.when(jnp.logical_or(k < PER_SLOT, upper))
        def _():
            z_own(k).start()

    def stage_y(k, g):
        @pl.when(g == 0)
        def _():
            z_own(k).wait()
            drain(zr.at[k, 0], SIDE * ON - 1)

        @pl.when(g == 1)
        def _():
            drain(zr.at[k, 1], SIDE * ON)

        for i in range(2):
            y_first(k, g, i).start()

    def stage_f(k, g):
        for i in range(2):
            y_first(k, g, i).wait_recv()
            y_second(k, g, i).start()

    def stage_s(k, g):
        for i in range(2):
            y_second(k, g, i).wait_recv()
        solve(k, g)

        @pl.loop(0, ON)
        def _(i):
            beside = lax.rem(o + i, ON)
            for r in range(SIDE):
                if r == 0:
                    @pl.when(g + i > 0)
                    def _():
                        m_out(k, g, r, beside).start()
                else:
                    m_out(k, g, r, beside).start()

        @pl.when(g == 0)
        def _():
            m_own(k).start()

    fold(0)
    widen(0)
    for fetch in fetches[2:]:
        fetch.start()
    tabulate(0)
    analyse(0, 0)
    pl.semaphore_wait(barrier, MA - 1 + 2)
    stage_z(0)
    stage_z(1)
    tabulate(1)
    analyse(0, 1)
    for k in range(2, PER_SLOT):
        stage_z(k)
    zeros[...] = jnp.zeros_like(zeros)
    fills = [pltpu.make_async_copy(zeros, out.at[1, n // HALVES, pl.ds(0, MA // 2), n % HALVES], fill.at[n]) for n in range(PER_SLOT)]
    for copy in fills:
        copy.start()
    stage_y(0, 0)
    fold(1)
    stage_y(0, 1)
    widen(1)
    tabulate(0)
    stage_f(0, 0)
    analyse(1, 0)
    stage_y(1, 0)
    stage_z(4)
    stage_z(5)
    stage_f(0, 1)
    tabulate(1)
    analyse(1, 1)
    stage_z(6)
    stage_z(7)
    fetches[2 * SLOTS].wait()

    @pl.loop(S_LAG, PIECES + S_LAG)
    def _(step):
        for stage_of, lag, first in ((stage_y, 0, 3), (stage_f, F_LAG, 2), (stage_s, S_LAG, 0)):
            t = step - lag
            k = t // GROUPS
            g = lax.rem(t + t // LAST, GROUPS)
            valid = jnp.logical_and(t >= first, t < PIECES)
            live = jnp.logical_or(k < PER_SLOT, upper)

            @pl.when(jnp.logical_and(valid, live))
            def _():
                stage_of(k, g)

    for copy in fills:
        copy.wait()

    @pl.loop(0, CHUNKS)
    def _(k):
        def returned():
            for g in range(GROUPS):
                for i in range(2):
                    y_first(k, g, i).wait_send()
                    y_second(k, g, i).wait_send()
            drain(ms.at[k], MA - 1)
            m_own(k).wait()

        @pl.when(k < PER_SLOT)
        def _():
            drain(zs.at[k], MA - 1)
            returned()
            drain(mr.at[k], MA - 1)

        @pl.when(jnp.logical_and(k >= PER_SLOT, upper))
        def _():
            drain(zs.at[k], MA // 2 - 1)
            returned()
            drain(mr.at[k], MA // 2 - 1)

        @pl.when(jnp.logical_and(k >= PER_SLOT, jnp.logical_not(upper)))
        def _():
            drain(zs.at[k], MA // 2)
            drain(mr.at[k], MA // 2)


def per_device(nonlinear, legendre, inverse, orders):
    tile = (ROWS, LANES)
    dma = pltpu.SemaphoreType.DMA
    field = nonlinear.reshape(SLOTS, 2 * THETA * PARTS, LANES)
    values = legendre.reshape(SLOTS, THETA, PARITIES, BLOCKS, LANES).transpose(0, 1, 3, 2, 4)
    values = values.reshape(SLOTS, THETA * BLOCKS * PARITIES, LANES)
    solved = pl.pallas_call(
        kernel,
        out_shape=jax.ShapeDtypeStruct((SLOTS, PARITIES, MA, HALVES) + tile, jnp.bfloat16),
        in_specs=[pl.BlockSpec(memory_space=pltpu.SMEM)] + [pl.BlockSpec(memory_space=pl.ANY)] * 3,
        out_specs=pl.BlockSpec(memory_space=pl.ANY),
        scratch_shapes=[
            pltpu.VMEM((SLOTS, 2) + field.shape[1:], jnp.bfloat16),
            pltpu.VMEM(field.shape[1:], jnp.float32),
            pltpu.VMEM((PARITIES, THETA, PARTS * LANES), jnp.bfloat16),
            pltpu.VMEM((PARITIES, THETA, DEGREES), jnp.bfloat16),
            pltpu.VMEM((DEGREES * PARTS, LANES), jnp.float32),
            pltpu.VMEM((SLOTS, PARITIES, MA, HALVES) + tile, jnp.bfloat16),
            pltpu.VMEM((CHUNKS, YN, GROUPS, SIDE, ON) + tile, jnp.bfloat16),
            pltpu.VMEM((CHUNKS, GROUPS, SIDE, ON) + tile, jnp.bfloat16),
            pltpu.VMEM(inverse.shape, jnp.bfloat16),
            pltpu.VMEM((MA // 2,) + tile, jnp.bfloat16),
            dma((CHUNKS,)), dma((CHUNKS, GROUPS)),
            dma((CHUNKS, GROUPS, 4)), dma((CHUNKS, GROUPS, 4)),
            dma((CHUNKS,)), dma((CHUNKS,)),
            dma((2, CHUNKS)),
            dma((2 * SLOTS + 1,)),
            dma((PER_SLOT,)),
        ],
        compiler_params=pltpu.CompilerParams(collective_id=0, has_side_effects=True, vmem_limit_bytes=50 * 1024 * 1024),
    )(orders, field, values, inverse)
    return solved.reshape(SLOTS, PARITIES, DEGREES, PARTS, LANES)


def solution(mesh):
    in_specs = (
        P("ma", None, None, "row"),
        P("ma", None, None, None),
        P(None, "ma", None, "row", None),
        P("ma"),
    )
    out_specs = P("ma", None, None, None, "row")
    return jax.shard_map(
        per_device, mesh=mesh, in_specs=in_specs, out_specs=out_specs, check_vma=False
    )
```

```python
import jax
import jax.numpy as jnp
from jax import lax
from jax.experimental import pallas as pl
from jax.experimental.pallas import tpu as pltpu
from jax.sharding import PartitionSpec as P

MESH = pl.DeviceIdType.MESH
NEAR, FAR = (0, 1, 7, 2), (6, 3, 5, 4)
OFFSETS = NEAR + FAR
GROUPS, SIDE = 2, 4
ZN, ON, YN = 8, 8, 4
MA = ZN * ON
SLOTS, PARITIES, HALVES, QUAD = 2, 2, 2, 4
PER_SLOT = PARITIES * HALVES
CHUNKS = SLOTS * PER_SLOT
ROWS, LANES = 16, 128
F_LAG, S_LAG = 1, 2
PIECES = CHUNKS * GROUPS
LAST = PIECES - GROUPS
PARTS = 4
THETA, FOLD = 768, 256
DEGREES = 512
BLOCKS = DEGREES // LANES


def kernel(orders, nonlinear, legendre, inverse, out,
           raw, wide, folded, table, stage, coef, gathered, solved, weights, zeros,
           zs, zr, ys, yr, ms, mr, own, load, fill):
    me = lax.axis_index("ma")
    y = lax.axis_index("row")
    z, o = me // ON, lax.rem(me, ON)
    upper = z >= ZN // 2

    def y_peer(i):
        return {"row": lax.rem(y + i, YN)}

    fetches = []
    for slot in range(SLOTS):
        fetches.append(pltpu.make_async_copy(nonlinear.at[slot], raw.at[slot, 0], load.at[2 * slot]))
        fetches.append(pltpu.make_async_copy(legendre.at[slot], raw.at[slot, 1], load.at[2 * slot + 1]))
    fetches.append(pltpu.make_async_copy(inverse, weights, load.at[2 * SLOTS]))
    for fetch in fetches[:2]:
        fetch.start()

    barrier = pltpu.get_barrier_semaphore()

    @pl.loop(1, MA)
    def _(i):
        pl.semaphore_signal(barrier, inc=1, device_id={"ma": lax.rem(me + i, MA)}, device_id_type=MESH)

    for i in (1, YN - 1):
        pl.semaphore_signal(barrier, inc=1, device_id=y_peer(i), device_id_type=MESH)

    def remote(src, dst, s, r, device):
        return pltpu.make_async_remote_copy(src_ref=src, dst_ref=dst, send_sem=s, recv_sem=r, device_id=device, device_id_type=MESH)

    def where(k):
        inner = k % PER_SLOT
        return k // PER_SLOT, inner // HALVES, inner % HALVES

    def z_out(k, q, beside):
        slot, p, h = where(k)
        away = (ZN - OFFSETS[q]) % ZN
        there = lax.rem(z + away, ZN) * ON + beside
        return remote(coef.at[slot, p, there, h], gathered.at[k, y, q // SIDE, q % SIDE, o], zs.at[k], zr.at[k, q // SIDE], {"ma": there})

    def z_own(k):
        slot, p, h = where(k)
        return pltpu.make_async_copy(coef.at[slot, p, me, h], gathered.at[k, y, 0, 0, o], own.at[0, k])

    def y_first(k, g, i):
        part = gathered.at[k, y, g]
        return remote(part, part, ys.at[k, g, i], yr.at[k, g, i], y_peer((1, YN - 1)[i]))

    def y_second(k, g, i):
        origin = lax.rem(y + (YN - 1, 1)[i], YN)
        part = gathered.at[k, origin, g, pl.ds((0, SIDE // 2)[i], SIDE // 2)]
        return remote(part, part, ys.at[k, g, 2 + i], yr.at[k, g, 2 + i], y_peer((1, YN - 1)[i]))

    def m_out(k, g, r, beside):
        slot, p, h = where(k)
        away = NEAR[r] + g * (FAR[r] - NEAR[r])
        there = lax.rem(z + away, ZN) * ON + beside
        return remote(solved.at[k, g, r, beside], out.at[slot, p, me, h], ms.at[k], mr.at[k], {"ma": there})

    def m_own(k):
        slot, p, h = where(k)
        return pltpu.make_async_copy(solved.at[k, 0, 0, o], out.at[slot, p, me, h], own.at[1, k])

    def drain(sem, count):
        part = coef.at[0, 0, pl.ds(0, count), 0]
        pltpu.make_async_copy(part, part, sem).wait()

    def fold(slot):
        fetches[2 * slot].wait()
        wide[...] = raw[slot, 0].astype(jnp.float32)
        index = lax.broadcasted_iota(jnp.int32, (FOLD, FOLD), 0) + lax.broadcasted_iota(jnp.int32, (FOLD, FOLD), 1)
        flip = (index == FOLD - 1).astype(jnp.bfloat16)
        sign = jnp.where(orders[slot] % 2 == 0, 1.0, -1.0).astype(jnp.float32)

        def rows(block):
            return [wide[pl.ds(block * FOLD * PARTS + c, FOLD, stride=PARTS), :] for c in range(PARTS)]

        for b in range(THETA // FOLD):
            north = jnp.concatenate(rows(b), axis=1)
            south = jnp.concatenate([v.astype(jnp.bfloat16) for v in rows(2 * THETA // FOLD - 1 - b)], axis=1)
            south = jnp.dot(flip, south, preferred_element_type=jnp.float32) * sign
            folded[0, b * FOLD:(b + 1) * FOLD, :] = (north + south).astype(jnp.bfloat16)
            folded[1, b * FOLD:(b + 1) * FOLD, :] = (north - south).astype(jnp.bfloat16)

    def widen(slot):
        fetches[2 * slot + 1].wait()
        wide[...] = raw[slot, 1].astype(jnp.float32)

    def tabulate(p):
        for b in range(BLOCKS):
            table[p, :, b * LANES:(b + 1) * LANES] = wide[pl.ds(b * PARITIES + p, THETA, stride=BLOCKS * PARITIES), :].astype(jnp.bfloat16)

    def analyse(slot, p):
        product = lax.dot_general(table[p], folded[p], (((0,), (0,)), ((), ())), preferred_element_type=jnp.float32)
        degree = 2 * lax.broadcasted_iota(jnp.int32, (DEGREES, 1), 0) + p
        product = jnp.where(degree >= orders[slot], product, 0.0)
        for c in range(PARTS):
            stage[pl.ds(c, DEGREES, stride=PARTS), :] = product[:, c * LANES:(c + 1) * LANES]
        coef[slot, p] = stage[...].astype(jnp.bfloat16).reshape(MA, HALVES, ROWS, LANES)

    def solve(k, g):
        slot, p, h = where(k)
        row = lax.broadcasted_iota(jnp.int32, (1, ROWS, LANES), 1)
        flat = gathered[k, :, g].reshape(YN, SIDE * ON * ROWS, LANES)
        left = jnp.concatenate([flat[n] for n in range(YN)], axis=1)
        total = None
        for jl in range(QUAD):
            right = weights[p, h * QUAD + jl].reshape(2 * LANES, YN * LANES)
            product = lax.dot_general(left, right, (((1,), (1,)), ((), ())), preferred_element_type=jnp.float32)
            product = product.reshape(SIDE * ON, ROWS, 2 * LANES)
            for f in range(2):
                piece = product[:, :, f * LANES:(f + 1) * LANES]
                total = piece if total is None else jnp.where(row // 2 == jl * 2 + f, piece, total)
        solved[k, g] = total.astype(jnp.bfloat16).reshape(SIDE, ON, ROWS, LANES)

    def stage_z(k):
        for g in range(GROUPS):
            @pl.loop(0, ON)
            def _(i):
                beside = lax.rem(o + i, ON)
                for r in range(SIDE):
                    q = g * SIDE + r
                    lands = lax.rem(z + (ZN - OFFSETS[q]) % ZN, ZN)
                    if k < PER_SLOT and q > 0:
                        z_out(k, q, beside).start()
                        continue
                    go = i > 0 if q == 0 else i >= 0
                    if k >= PER_SLOT:
                        go = jnp.logical_and(go, lands >= ZN // 2)

                    @pl.when(go)
                    def _():
                        z_out(k, q, beside).start()

        @pl.when(jnp.logical_or(k < PER_SLOT, upper))
        def _():
            z_own(k).start()

    def stage_y(k, g):
        @pl.when(g == 0)
        def _():
            z_own(k).wait()
            drain(zr.at[k, 0], SIDE * ON - 1)

        @pl.when(g == 1)
        def _():
            drain(zr.at[k, 1], SIDE * ON)

        for i in range(2):
            y_first(k, g, i).start()

    def stage_f(k, g):
        for i in range(2):
            y_first(k, g, i).wait_recv()
            y_second(k, g, i).start()

    def stage_s(k, g):
        for i in range(2):
            y_second(k, g, i).wait_recv()
        solve(k, g)

        @pl.loop(0, ON)
        def _(i):
            beside = lax.rem(o + i, ON)
            for r in range(SIDE):
                if r == 0:
                    @pl.when(g + i > 0)
                    def _():
                        m_out(k, g, r, beside).start()
                else:
                    m_out(k, g, r, beside).start()

        @pl.when(g == 0)
        def _():
            m_own(k).start()

    fold(0)
    widen(0)
    for fetch in fetches[2:]:
        fetch.start()
    tabulate(0)
    analyse(0, 0)
    pl.semaphore_wait(barrier, MA - 1 + 2)
    stage_z(0)
    stage_z(1)
    tabulate(1)
    analyse(0, 1)
    for k in range(2, PER_SLOT):
        stage_z(k)
    zeros[...] = jnp.zeros_like(zeros)
    fills = [pltpu.make_async_copy(zeros, out.at[1, n // HALVES, pl.ds(0, MA // 2), n % HALVES], fill.at[n]) for n in range(PER_SLOT)]
    for copy in fills:
        copy.start()
    stage_y(0, 0)
    fold(1)
    stage_y(0, 1)
    widen(1)
    tabulate(0)
    stage_f(0, 0)
    analyse(1, 0)
    stage_y(1, 0)
    stage_z(4)
    stage_z(5)
    stage_f(0, 1)
    tabulate(1)
    analyse(1, 1)
    stage_z(6)
    stage_z(7)
    fetches[2 * SLOTS].wait()

    @pl.loop(S_LAG, PIECES + S_LAG)
    def _(step):
        for stage_of, lag, first in ((stage_y, 0, 3), (stage_f, F_LAG, 2), (stage_s, S_LAG, 0)):
            t = step - lag
            k = t // GROUPS
            g = lax.rem(t + t // LAST, GROUPS)
            valid = jnp.logical_and(t >= first, t < PIECES)
            live = jnp.logical_or(k < PER_SLOT, upper)

            @pl.when(jnp.logical_and(valid, live))
            def _():
                stage_of(k, g)

    for copy in fills:
        copy.wait()

    @pl.loop(0, CHUNKS)
    def _(k):
        def returned():
            for g in range(GROUPS):
                for i in range(2):
                    y_first(k, g, i).wait_send()
                    y_second(k, g, i).wait_send()
            drain(ms.at[k], MA - 1)
            m_own(k).wait()

        @pl.when(k < PER_SLOT)
        def _():
            drain(zs.at[k], MA - 1)
            returned()
            drain(mr.at[k], MA - 1)

        @pl.when(jnp.logical_and(k >= PER_SLOT, upper))
        def _():
            drain(zs.at[k], MA // 2 - 1)
            returned()
            drain(mr.at[k], MA // 2 - 1)

        @pl.when(jnp.logical_and(k >= PER_SLOT, jnp.logical_not(upper)))
        def _():
            drain(zs.at[k], MA // 2)
            drain(mr.at[k], MA // 2)


def per_device(nonlinear, legendre, inverse, orders):
    tile = (ROWS, LANES)
    dma = pltpu.SemaphoreType.DMA
    field = nonlinear.reshape(SLOTS, 2 * THETA * PARTS, LANES)
    values = legendre.reshape(SLOTS, THETA, PARITIES, BLOCKS, LANES).transpose(0, 1, 3, 2, 4)
    values = values.reshape(SLOTS, THETA * BLOCKS * PARITIES, LANES)
    solved = pl.pallas_call(
        kernel,
        out_shape=jax.ShapeDtypeStruct((SLOTS, PARITIES, MA, HALVES) + tile, jnp.bfloat16),
        in_specs=[pl.BlockSpec(memory_space=pltpu.SMEM)] + [pl.BlockSpec(memory_space=pl.ANY)] * 3,
        out_specs=pl.BlockSpec(memory_space=pl.ANY),
        scratch_shapes=[
            pltpu.VMEM((SLOTS, 2) + field.shape[1:], jnp.bfloat16),
            pltpu.VMEM(field.shape[1:], jnp.float32),
            pltpu.VMEM((PARITIES, THETA, PARTS * LANES), jnp.bfloat16),
            pltpu.VMEM((PARITIES, THETA, DEGREES), jnp.bfloat16),
            pltpu.VMEM((DEGREES * PARTS, LANES), jnp.float32),
            pltpu.VMEM((SLOTS, PARITIES, MA, HALVES) + tile, jnp.bfloat16),
            pltpu.VMEM((CHUNKS, YN, GROUPS, SIDE, ON) + tile, jnp.bfloat16),
            pltpu.VMEM((CHUNKS, GROUPS, SIDE, ON) + tile, jnp.bfloat16),
            pltpu.VMEM(inverse.shape, jnp.bfloat16),
            pltpu.VMEM((MA // 2,) + tile, jnp.bfloat16),
            dma((CHUNKS,)), dma((CHUNKS, GROUPS)),
            dma((CHUNKS, GROUPS, 4)), dma((CHUNKS, GROUPS, 4)),
            dma((CHUNKS,)), dma((CHUNKS,)),
            dma((2, CHUNKS)),
            dma((2 * SLOTS + 1,)),
            dma((PER_SLOT,)),
        ],
        compiler_params=pltpu.CompilerParams(collective_id=0, has_side_effects=True, vmem_limit_bytes=50 * 1024 * 1024),
    )(orders, field, values, inverse)
    return solved.reshape(SLOTS, PARITIES, DEGREES, PARTS, LANES)


def solution(mesh):
    in_specs = (
        P("ma", None, None, "row"),
        P("ma", None, None, None),
        P(None, "ma", None, "row", None),
        P("ma"),
    )
    out_specs = P("ma", None, None, None, "row")
    return jax.shard_map(
        per_device, mesh=mesh, in_specs=in_specs, out_specs=out_specs, check_vma=False
    )
```
